512 devices in a mesh: row: 32 (over y, x, core), col: 16 (over z).
Axes of the slice: x: 4, y: 4, z: 16, core: 2. Of those that a mesh axis runs over, the one named last changes fastest.
Arguments:
- points: float32 [65536, 128], P(('row', 'col')), may hold values from -6 to 6
- lengthscales: float32 [128], replicated, may hold values from 3.0547013 to 5.9962654
- noise: float32 [65536], P(('row', 'col')), may hold values from 0.5 to 2
- targets: float32 [32, 65536], P(None, ('row', 'col')), may hold values from -6 to 6
Outputs:
- solution: float32 [32, 65536], P(None, ('row', 'col'))
- residual: float32 [32, 65536], P(None, ('row', 'col'))
- direction: float32 [32, 65536], P(None, ('row', 'col'))
The draws below stay inside these ranges and needn't reach their ends.
All inputs are finite; a program needn't handle non-finite values.
Results may differ from the reference program's by a relative error of at most 0.0077.
Values may be sent and summed in bfloat16 or wider, within the bound.
A program may use at most 64 MiB of HBM per device.

```python
import math
import jax
import jax.numpy as jnp
from jax import lax

D = 128
R = 32
N = 65536


def block_levels(key, shape, shards, low, high):
    loudness, own = 1.0, jax.random.fold_in(key, 6)
    for position, blocks in shards:
        draws = jnp.exp(jax.random.uniform(jax.random.fold_in(own, position), (blocks,), jnp.float32, low / len(shards), high / len(shards)))
        loudness = loudness * jnp.repeat(draws, shape[position] // blocks).reshape([-1 if axis == position else 1 for axis in range(len(shape))])
    return loudness


def normal_values(key, extent, width, most, cuts=(), kind=jnp.bfloat16):
    entries = jax.random.normal(key, extent, jnp.float32) * width
    if len(cuts) > 0:
        entries = block_levels(key, extent, cuts, -0.22, 0.18) * entries
    return jnp.clip(entries, min=-most, max=most).astype(kind)


def setup_inputs(seed: int = 0) -> dict:
    seeds = jax.random.split(jax.random.key(seed), 5)
    points = normal_values(seeds[0], (N, D), 1.0, 6.0, ((0, 512),), jnp.float32)
    lengthscales = jnp.clip(jnp.exp(jax.random.uniform(seeds[1], (D,), jnp.float32, math.log(3.0547013), math.log(5.9962654))), 3.0547013, 5.9962654)
    noise = jnp.clip(0.5 + 1.5 * jax.random.uniform(seeds[2], (N,), jnp.float32) ** block_levels(seeds[2], (N,), ((0, 512),), -0.2, 0.2), 0.5, 2.0)
    targets = normal_values(seeds[3], (R, N), 1.0, 6.0, ((1, 512),), jnp.float32)
    return dict(points=points, lengthscales=lengthscales, noise=noise, targets=targets)


root_five = 5.0 ** 0.5

def chol_solve(matrix, rhs):
    return jax.scipy.linalg.cho_solve((jnp.linalg.cholesky(matrix), True), rhs)

def matern(left, left_sq, right, right_sq):
    cross = jnp.dot(left.astype(jnp.float32), right.astype(jnp.float32).T.astype(jnp.float32), preferred_element_type=jnp.float32)
    dist_sq = jnp.maximum(left_sq[:, None] + right_sq[None, :] - 2.0 * cross, 0.0)
    dist = jnp.sqrt(dist_sq)
    value = (1.0 + root_five * dist + 5.0 / 3.0 * dist_sq) * jnp.exp(-root_five * dist)
    return value.astype(jnp.bfloat16)

def reference(points, lengthscales, noise, targets):
    precise = lax.Precision.HIGHEST
    scaled = (points / lengthscales[None, :]).astype(jnp.bfloat16)
    sqnorm = lax.optimization_barrier(jnp.sum(jnp.square(scaled.astype(jnp.float32)), axis=1))
    dir_half = targets.astype(jnp.bfloat16)
    block_rows = math.gcd(N, 512)

    def row_block(index):
        begin = index * block_rows
        rows = lax.dynamic_slice_in_dim(scaled, begin, block_rows, 0)
        rows_sq = lax.dynamic_slice_in_dim(sqnorm, begin, block_rows, 0)
        tile = matern(rows, rows_sq, scaled, sqnorm)
        return jnp.dot(dir_half.astype(jnp.float32), tile.astype(jnp.float32).T.astype(jnp.float32), preferred_element_type=jnp.float32)
    blocks = lax.map(row_block, jnp.arange(N // block_rows, dtype=jnp.int32))
    image = jnp.transpose(blocks, (1, 0, 2)).reshape(R, N) + noise[None, :] * targets
    first = jnp.dot(targets, targets.T, precision=precise)
    curvature = jnp.dot(targets, image.T, precision=precise)
    step_matrix = chol_solve(curvature, first)
    solution = jnp.dot(step_matrix.T, targets, precision=precise)
    residual = targets - jnp.dot(step_matrix.T, image, precision=precise)
    norm_new = jnp.dot(residual, residual.T, precision=precise)
    ratio = chol_solve(first, norm_new)
    direction = residual + jnp.dot(ratio.T, targets, precision=precise)
    return (solution, residual, direction)
```

```python
import functools

import jax
import jax.numpy as jnp
from jax import lax
from jax.experimental import pallas as pl
from jax.experimental.pallas import tpu as pltpu
from jax.sharding import PartitionSpec as P

MESH = pl.DeviceIdType.MESH
HI = lax.Precision.HIGHEST
root_five = 5.0**0.5
log2_e = 1.4426950408889634

PLANE = 16
RING = 16
BLOCK = 128
RHS = 32
DIRECT = (6, -6, 3, -3, 1, -1)
NEAR = (0,) + DIRECT
FAR = (2, -2, 4, -4, 5, -5, 7, -7, 8)
OFFSETS = NEAR + FAR
FORWARD = {6: (1, -1, 2), -6: (1, -1), 3: (1, -1), -3: (1, -1), 1: (), -1: ()}
PAIR = 2 * BLOCK


def place():
    row, col = lax.axis_index("row"), lax.axis_index("col")
    return lax.div(row, 8), lax.rem(lax.div(row, 2), 4), lax.rem(row, 2), col


def in_plane(step):
    y, x, core, z = place()
    y = lax.rem(y + lax.div(step, 4), 4)
    x = lax.rem(x + lax.rem(step, 4), 4)
    return (y * 8 + x * 2 + core, z)


def back(step):
    return lax.rem(4 - lax.div(step, 4), 4) * 4 + lax.rem(4 - lax.rem(step, 4), 4)


def along_z(step):
    y, x, core, z = place()
    return (y * 8 + x * 2 + core, lax.rem(z + (step + RING), RING))


def other_core():
    y, x, core, z = place()
    return (y * 8 + x * 2 + 1 - core, z)


def remote(src, dst, send, recv, device):
    return pltpu.make_async_remote_copy(
        src_ref=src, dst_ref=dst, send_sem=send, recv_sem=recv, device_id=device, device_id_type=MESH
    )


def landed(ref, sem):
    pltpu.make_async_copy(ref, ref, sem).wait()


def split_norms(rows):
    wide = rows.astype(jnp.float32)
    norm = jnp.sum(wide * wide, axis=1, keepdims=True)
    high = norm.astype(jnp.bfloat16).astype(jnp.float32)
    rest = norm - high
    middle = rest.astype(jnp.bfloat16).astype(jnp.float32)
    return high, middle, rest - middle


def norm_lanes(rows, first):
    high, middle, low = split_norms(rows)
    lane = lax.broadcasted_iota(jnp.int32, rows.shape, 1)
    ones = 3 - first
    value = jnp.where((lane >= ones) & (lane < ones + 3), 1.0, 0.0)
    value = jnp.where(lane == first, high, value)
    value = jnp.where(lane == first + 1, middle, value)
    return jnp.where(lane == first + 2, low, value).astype(jnp.bfloat16)


def matern(dist_sq):
    dist_sq = jnp.maximum(dist_sq, 1e-30)
    dist = dist_sq * lax.rsqrt(dist_sq)
    decay = jnp.exp2(dist * (-root_five * log2_e))
    return (((5.0 / 3.0 * dist_sq + 1.0) + root_five * dist) * decay).astype(jnp.bfloat16)


def product(dirs, rows, norms, out_points):
    dist_sq = lax.dot_general(
        jnp.concatenate([rows, norms], axis=1), out_points, (((1,), (1,)), ((), ())), preferred_element_type=jnp.float32
    )
    return jnp.dot(dirs, matern(dist_sq), preferred_element_type=jnp.float32)


def eliminate(matrix):
    row = lax.broadcasted_iota(jnp.int32, matrix.shape, 0)
    for k in range(RHS):
        pivot = matrix[k : k + 1, :] / matrix[k : k + 1, k : k + 1]
        matrix = jnp.where(row == k, pivot, matrix - matrix[:, k : k + 1] * pivot)
    return matrix


def shift(value, lanes):
    return pltpu.roll(value, lanes % 128, 1)


def precise(left, right):
    return jnp.dot(left, right, precision=HI, preferred_element_type=jnp.float32)


def gram(left, right):
    return lax.dot_general(left, right, (((1,), (1,)), ((), ())), precision=HI, preferred_element_type=jnp.float32)


def pack(rows):
    lane = lax.broadcasted_iota(jnp.int32, (8, 128), 1)
    return jnp.where(lane < 64, rows[0:8], shift(rows[8:16], 64))


def wide(value):
    return jnp.concatenate([value, jnp.zeros((value.shape[0], 128 - value.shape[1]), value.dtype)], axis=1)


class Sum:
    def __init__(self, parts, plane, ring, halves, sems):
        self.parts, self.plane, self.ring, self.halves = parts, plane, ring, halves
        self.core_send, self.core_recv, self.plane_send, self.plane_recv, self.ring_send, self.ring_recv = sems

    def begin(self, value):
        core = place()[2]
        first, second = pack(value[0:16]), pack(value[16:32])
        low = core == 0
        self.parts[0] = jnp.where(low, first, second)
        self.parts[1] = jnp.where(low, second, first)
        remote(self.parts.at[1], self.parts.at[2], self.core_send.at[0], self.core_recv.at[0], other_core()).start()

    def over_plane(self):
        y, x, _, _ = place()
        me = y * 4 + x
        landed(self.parts.at[2], self.core_recv.at[0])
        self.plane[me] = self.parts[0] + self.parts[2]

        def send(k, _):
            remote(self.plane.at[me], self.plane.at[me], self.plane_send.at[k], self.plane_recv, in_plane(k)).start()
            return 0

        lax.fori_loop(1, PLANE, send, 0, unroll=True)

    def over_ring(self):
        me = place()[3]
        landed(self.plane.at[pl.ds(1, PLANE - 1)], self.plane_recv)
        self.ring[me] = jnp.sum(self.plane[...], axis=0)
        for k in (8, -7, 7, -6, 6, -5, 5, -4, 4, -3, 3, -2, 2, -1, 1):
            remote(self.ring.at[me], self.ring.at[me], self.ring_send.at[k % RING], self.ring_recv, along_z(k)).start()

    def over_cores(self):
        core = place()[2]
        landed(self.ring.at[pl.ds(1, RING - 1)], self.ring_recv)
        self.halves[core] = jnp.sum(self.ring[...], axis=0)
        remote(self.halves.at[core], self.halves.at[core], self.core_send.at[1], self.core_recv.at[1], other_core()).start()

    def end(self):
        landed(self.halves.at[0], self.core_recv.at[1])
        first, second = self.halves[0], self.halves[1]
        return jnp.concatenate([first, shift(first, 64), second, shift(second, 64)], axis=0)

    def sent(self):
        landed(self.parts.at[1], self.core_send.at[0])
        landed(self.halves.at[0], self.core_send.at[1])
        for k in range(1, PLANE):
            landed(self.plane.at[0], self.plane_send.at[k])
        for k in range(1, RING):
            landed(self.ring.at[0], self.ring_send.at[k])


def kernel(
    points, scales, noise, targets, solution_ref, residual_ref, direction_ref,
    near_far, norms, out_raw, out_points, own, total, outbox, inbox,
    parts_a, plane_a, ring_a, halves_a, parts_b, plane_b, ring_b, halves_b,
    in_send, in_recv, across_send, across_recv, forward_send, out_send, out_recv, box_send, box_recv,
    cs_a, cr_a, ps_a, pr_a, rs_a, rr_a, cs_b, cr_b, ps_b, pr_b, rs_b, rr_b,
):
    barrier = pltpu.get_barrier_semaphore()

    def greet(device):
        pl.semaphore_signal(barrier, inc=1, device_id=device, device_id_type=MESH)

    def greet_plane(k, _):
        greet(in_plane(k))
        return 0

    for k in (8, -7, 7, -6, 6, -5, 5, -4, 4, -3, 3, -2, 2, -1, 1):
        greet(along_z(k))
    lax.fori_loop(1, PLANE, greet_plane, 0, unroll=True)
    greet(other_core())

    goals = targets[...]
    scaled = (points[...] / scales[...]).astype(jnp.bfloat16)
    own[...] = scaled
    near_far[0, 0:BLOCK] = scaled
    near_far[0, BLOCK : BLOCK + RHS] = goals.astype(jnp.bfloat16)
    norms[0:BLOCK] = norm_lanes(scaled, 0)
    out_points[15 * BLOCK : 16 * BLOCK, 0:BLOCK] = scaled * -2.0
    out_points[15 * BLOCK : 16 * BLOCK, BLOCK:PAIR] = norm_lanes(scaled, 3)
    first_sum = Sum(parts_a, plane_a, ring_a, halves_a, (cs_a, cr_a, ps_a, pr_a, rs_a, rr_a))
    last_sum = Sum(parts_b, plane_b, ring_b, halves_b, (cs_b, cr_b, ps_b, pr_b, rs_b, rr_b))
    first_part = wide(gram(goals, goals))

    pl.semaphore_wait(barrier, (RING - 1) + (PLANE - 1) + 1)

    for i, step in enumerate(OFFSETS):
        if step in DIRECT:
            remote(near_far.at[0], near_far.at[2 * i], in_send.at[i], in_recv.at[i], along_z(step)).start()

    def across(i):
        remote(near_far.at[2 * i], near_far.at[2 * i + 1], across_send.at[i], across_recv.at[i], other_core()).start()

    def send_out(k, _):
        slot = 15 - back(k)
        remote(own, out_raw.at[slot], out_send.at[k], out_recv.at[slot], in_plane(k)).start()
        return 0

    lax.fori_loop(1, PLANE, send_out, 0, unroll=True)
    across(0)
    first_sum.begin(first_part)

    def arrived(i):
        landed(near_far.at[2 * i], in_recv.at[i])
        across(i)

    def take(slot):
        norms[slot * BLOCK : (slot + 1) * BLOCK] = norm_lanes(near_far[slot, 0:BLOCK], 0)

    forwards = []
    for step in (1, -1, 3, -3, 6, -6):
        i = OFFSETS.index(step)
        arrived(i)
        for more in FORWARD[step]:
            j = OFFSETS.index(step + more)
            n = len(forwards)
            forwards.append(j)
            remote(near_far.at[2 * i], near_far.at[2 * j], forward_send.at[n], in_recv.at[j], along_z(more)).start()
        take(2 * i)
    first_sum.over_plane()

    def take_out(slot, _):
        landed(out_raw.at[slot], out_recv.at[slot])
        rows = out_raw[slot]
        at = pl.ds(pl.multiple_of(slot * BLOCK, BLOCK), BLOCK)
        out_points[at, 0:BLOCK] = rows * -2.0
        out_points[at, BLOCK:PAIR] = norm_lanes(rows, 3)
        return 0

    lax.fori_loop(0, PLANE - 1, take_out, 0)

    def take_across(i):
        landed(near_far.at[2 * i + 1], across_recv.at[i])
        take(2 * i + 1)

    for i in range(len(NEAR)):
        take_across(i)

    def partial(begin, end, o):
        rows = near_far[begin:end, 0:BLOCK].reshape((end - begin) * BLOCK, BLOCK)
        dirs = jnp.concatenate([near_far[s, BLOCK : BLOCK + RHS] for s in range(begin, end)], axis=1)
        at = pl.ds(pl.multiple_of(o * PAIR, PAIR), PAIR)
        return product(dirs, rows, norms[begin * BLOCK : end * BLOCK], out_points[at, :])

    near_slots, slots = 2 * len(NEAR), 2 * len(OFFSETS)

    def near_part(o, _):
        total[o] = partial(0, near_slots, o)
        return 0

    lax.fori_loop(0, PLANE // 2, near_part, 0)

    for i in range(len(NEAR), len(OFFSETS)):
        arrived(i)
        take(2 * i)
    first_sum.over_ring()
    for i in range(len(NEAR), len(OFFSETS)):
        take_across(i)

    def far_part(o, _):
        value = total[o] + partial(near_slots, slots, o)
        outbox[2 * o] = value[:, 0:BLOCK]
        outbox[2 * o + 1] = value[:, BLOCK:PAIR]

        def post(slot):
            step = 15 - slot
            remote(outbox.at[slot], inbox.at[slot], box_send.at[slot], box_recv, in_plane(step)).start()

        post(2 * o)

        @pl.when(o < PLANE // 2 - 1)
        def _():
            post(2 * o + 1)

        return 0

    lax.fori_loop(0, PLANE // 2, far_part, 0)
    first_sum.over_cores()

    lane = lax.broadcasted_iota(jnp.int32, (RHS, 128), 1)
    row = lax.broadcasted_iota(jnp.int32, (RHS, 128), 0)
    first = jnp.where(lane < RHS, first_sum.end(), 0.0)
    identity = jnp.where(lane == row + RHS, 1.0, 0.0)
    first_inverse = shift(eliminate(first + identity), -RHS)[:, 0:RHS]

    landed(inbox.at[pl.ds(0, PLANE - 1)], box_recv)
    image = (jnp.sum(inbox[0 : PLANE - 1], axis=0) + outbox[PLANE - 1]) + noise[...] * goals

    last_sum.begin(wide(gram(image, jnp.concatenate([goals, image], axis=0))))
    last_sum.over_plane()
    last_sum.over_ring()
    last_sum.over_cores()
    sums = last_sum.end()
    turned = sums[:, 0:RHS]
    curvature = wide(0.5 * (turned + turned.T))
    solved = eliminate(curvature + shift(first, RHS))
    step_matrix = shift(solved, -RHS)[:, 0:RHS]
    step_turned = step_matrix.T
    moved = precise(step_turned, jnp.concatenate([goals, image], axis=1))
    residual = goals - moved[:, 128:256]
    solution_ref[...] = moved[:, 0:128]
    residual_ref[...] = residual
    both = precise(step_turned, sums)
    cross = both[:, 0:RHS]
    square = precise(shift(both, -RHS)[:, 0:RHS], step_matrix)
    norm_new = first[:, 0:RHS] - cross - cross.T + square
    ratio_turned = precise(norm_new, first_inverse)
    direction_ref[...] = residual + precise(ratio_turned, goals)

    for i, step in enumerate(OFFSETS):
        if step in DIRECT:
            landed(near_far.at[0], in_send.at[i])
        landed(near_far.at[0], across_send.at[i])
    for n in range(len(forwards)):
        landed(near_far.at[0], forward_send.at[n])
    for k in range(1, PLANE):
        landed(own, out_send.at[k])
        landed(outbox.at[0], box_send.at[k - 1])
    first_sum.sent()
    last_sum.sent()


def per_device(points, lengthscales, noise, targets):
    vmem = pl.BlockSpec(memory_space=pltpu.VMEM)
    out = jax.ShapeDtypeStruct((RHS, BLOCK), jnp.float32)
    dma = pltpu.SemaphoreType.DMA
    sums = [
        pltpu.VMEM((3, 8, 128), jnp.float32),
        pltpu.VMEM((PLANE, 8, 128), jnp.float32),
        pltpu.VMEM((RING, 8, 128), jnp.float32),
        pltpu.VMEM((2, 8, 128), jnp.float32),
    ]
    sum_sems = [dma((2,)), dma((2,)), dma((PLANE,)), dma, dma((RING,)), dma]
    slots = 2 * len(OFFSETS)
    return pl.pallas_call(
        kernel,
        out_shape=(out, out, out),
        in_specs=[vmem] * 4,
        out_specs=(vmem,) * 3,
        scratch_shapes=[
            pltpu.VMEM((slots, BLOCK + RHS, BLOCK), jnp.bfloat16),
            pltpu.VMEM((slots * BLOCK, BLOCK), jnp.bfloat16),
            pltpu.VMEM((PLANE, BLOCK, BLOCK), jnp.bfloat16),
            pltpu.VMEM((PLANE * BLOCK, PAIR), jnp.bfloat16),
            pltpu.VMEM((BLOCK, BLOCK), jnp.bfloat16),
            pltpu.VMEM((PLANE // 2, RHS, PAIR), jnp.float32),
            pltpu.VMEM((PLANE, RHS, BLOCK), jnp.float32),
            pltpu.VMEM((PLANE, RHS, BLOCK), jnp.float32),
            *sums,
            *sums,
            dma((len(OFFSETS),)),
            dma((len(OFFSETS),)),
            dma((len(OFFSETS),)),
            dma((len(OFFSETS),)),
            dma((16,)),
            dma((PLANE,)),
            dma((PLANE,)),
            dma((PLANE,)),
            dma,
            *sum_sems,
            *sum_sems,
        ],
        compiler_params=pltpu.CompilerParams(collective_id=0, has_side_effects=True, vmem_limit_bytes=48 << 20),
        cost_estimate=pl.CostEstimate(flops=3 << 30, bytes_accessed=1 << 20, transcendentals=1 << 24),
        name="step",
    )(points, lengthscales[None, :], noise[None, :], targets)


def solution(mesh):
    spread = P(None, ("row", "col"))
    return jax.shard_map(
        per_device,
        mesh=mesh,
        in_specs=(P(("row", "col"), None), P(), P(("row", "col")), spread),
        out_specs=(spread, spread, spread),
        check_vma=False,
    )
```

```python
import functools

import jax
import jax.numpy as jnp
from jax import lax
from jax.experimental import pallas as pl
from jax.experimental.pallas import tpu as pltpu
from jax.sharding import PartitionSpec as P

MESH = pl.DeviceIdType.MESH
HI = lax.Precision.HIGHEST
root_five = 5.0**0.5
log2_e = 1.4426950408889634

PLANE = 16
RING = 16
BLOCK = 128
RHS = 32
DIRECT = (3, -3, 1, -1)
NEAR = (0, 1, -1, 3, -3)
MIDDLE = (2, -2, 4, -4, 6, -6)
FAR = (5, -5, 7, -7, 8)
OFFSETS = NEAR + MIDDLE + FAR
FORWARD = {3: (3, 1, -1), -3: (-3, -1, 1), 6: (2, 1, -1), -6: (-1, 1)}
PAIR = 2 * BLOCK
PAIRS = PLANE // 2


def place():
    row, col = lax.axis_index("row"), lax.axis_index("col")
    return lax.div(row, 8), lax.rem(lax.div(row, 2), 4), lax.rem(row, 2), col


def in_plane(step):
    y, x, core, z = place()
    y = lax.rem(y + lax.div(step, 4), 4)
    x = lax.rem(x + lax.rem(step, 4), 4)
    return (y * 8 + x * 2 + core, z)


def back(step):
    return lax.rem(4 - lax.div(step, 4), 4) * 4 + lax.rem(4 - lax.rem(step, 4), 4)


def along_z(step):
    y, x, core, z = place()
    return (y * 8 + x * 2 + core, lax.rem(z + (step + RING), RING))


def other_core():
    y, x, core, z = place()
    return (y * 8 + x * 2 + 1 - core, z)


def remote(src, dst, send, recv, device):
    return pltpu.make_async_remote_copy(
        src_ref=src, dst_ref=dst, send_sem=send, recv_sem=recv, device_id=device, device_id_type=MESH
    )


def landed(ref, sem):
    pltpu.make_async_copy(ref, ref, sem).wait()


def split_norms(rows):
    wide = rows.astype(jnp.float32)
    norm = jnp.sum(wide * wide, axis=1, keepdims=True)
    high = norm.astype(jnp.bfloat16).astype(jnp.float32)
    rest = norm - high
    middle = rest.astype(jnp.bfloat16).astype(jnp.float32)
    return high, middle, rest - middle


def norm_lanes(rows, first):
    high, middle, low = split_norms(rows)
    lane = lax.broadcasted_iota(jnp.int32, rows.shape, 1)
    ones = 3 - first
    value = jnp.where((lane >= ones) & (lane < ones + 3), 1.0, 0.0)
    value = jnp.where(lane == first, high, value)
    value = jnp.where(lane == first + 1, middle, value)
    return jnp.where(lane == first + 2, low, value).astype(jnp.bfloat16)


def matern(dist_sq):
    dist_sq = jnp.maximum(dist_sq, 1e-30)
    dist = dist_sq * lax.rsqrt(dist_sq)
    decay = jnp.exp2(dist * (-root_five * log2_e))
    return (((5.0 / 3.0 * dist_sq + 1.0) + root_five * dist) * decay).astype(jnp.bfloat16)


def distances(rows, norms, out_points):
    return lax.dot_general(
        jnp.concatenate([rows, norms], axis=1), out_points, (((1,), (1,)), ((), ())), preferred_element_type=jnp.float32
    )


def eliminate(matrix):
    parts = [matrix[8 * i : 8 * i + 8] for i in range(RHS // 8)]
    row = lax.broadcasted_iota(jnp.int32, parts[0].shape, 0)
    for k in range(0, RHS, 2):
        q, r = k // 8, k % 8
        left = [jnp.broadcast_to(part[:, k : k + 1], part.shape) for part in parts]
        right = [jnp.broadcast_to(part[:, k + 1 : k + 2], part.shape) for part in parts]
        upper, lower = parts[q][r : r + 1], parts[q][r + 1 : r + 2]
        a, b = left[q][r : r + 1], right[q][r : r + 1]
        c, d = left[q][r + 1 : r + 2], right[q][r + 1 : r + 2]
        scale = 1.0 / (a * d - b * c)
        upper, lower = (d * upper - b * lower) * scale, (a * lower - c * upper) * scale
        parts = [part - x * upper - y * lower for part, x, y in zip(parts, left, right)]
        parts[q] = jnp.where(row == r, upper, jnp.where(row == r + 1, lower, parts[q]))
    return jnp.concatenate(parts, axis=0)


def shift(value, lanes):
    return pltpu.roll(value, lanes % 128, 1)


def precise(left, right):
    return jnp.dot(left, right, precision=HI, preferred_element_type=jnp.float32)


def gram(left, right):
    return lax.dot_general(left, right, (((1,), (1,)), ((), ())), precision=HI, preferred_element_type=jnp.float32)


def pack(rows):
    lane = lax.broadcasted_iota(jnp.int32, (8, 128), 1)
    return jnp.where(lane < 64, rows[0:8], shift(rows[8:16], 64))


def wide(value):
    return jnp.concatenate([value, jnp.zeros((value.shape[0], 128 - value.shape[1]), value.dtype)], axis=1)


class Sum:
    def __init__(self, parts, plane, ring, halves, sems):
        self.parts, self.plane, self.ring, self.halves = parts, plane, ring, halves
        self.core_send, self.core_recv, self.plane_send, self.plane_recv, self.ring_send, self.ring_recv = sems

    def begin(self, value):
        core = place()[2]
        first, second = pack(value[0:16]), pack(value[16:32])
        low = core == 0
        self.parts[0] = jnp.where(low, first, second)
        self.parts[1] = jnp.where(low, second, first)
        remote(self.parts.at[1], self.parts.at[2], self.core_send.at[0], self.core_recv.at[0], other_core()).start()

    def over_plane(self):
        y, x, _, _ = place()
        me = y * 4 + x
        landed(self.parts.at[2], self.core_recv.at[0])
        self.plane[me] = self.parts[0] + self.parts[2]

        def send(k, _):
            remote(self.plane.at[me], self.plane.at[me], self.plane_send.at[k], self.plane_recv, in_plane(k)).start()
            return 0

        lax.fori_loop(1, PLANE, send, 0, unroll=True)

    def over_ring(self):
        me = place()[3]
        landed(self.plane.at[pl.ds(1, PLANE - 1)], self.plane_recv)
        self.ring[me] = jnp.sum(self.plane[...], axis=0)
        for k in (8, -7, 7, -6, 6, -5, 5, -4, 4, -3, 3, -2, 2, -1, 1):
            remote(self.ring.at[me], self.ring.at[me], self.ring_send.at[k % RING], self.ring_recv, along_z(k)).start()

    def over_cores(self):
        core = place()[2]
        landed(self.ring.at[pl.ds(1, RING - 1)], self.ring_recv)
        self.halves[core] = jnp.sum(self.ring[...], axis=0)
        remote(self.halves.at[core], self.halves.at[core], self.core_send.at[1], self.core_recv.at[1], other_core()).start()

    def end(self):
        landed(self.halves.at[0], self.core_recv.at[1])
        first, second = self.halves[0], self.halves[1]
        return jnp.concatenate([first, shift(first, 64), second, shift(second, 64)], axis=0)

    def sent(self):
        landed(self.parts.at[1], self.core_send.at[0])
        landed(self.halves.at[0], self.core_send.at[1])
        for k in range(1, PLANE):
            landed(self.plane.at[0], self.plane_send.at[k])
        for k in range(1, RING):
            landed(self.ring.at[0], self.ring_send.at[k])


def kernel(
    points_in, scales_in, noise_in, targets_in, out_ref,
    points, scales, noise, targets, dist_sq, near_far, norms, out_raw, out_points, own, total, outbox, inbox,
    parts_a, plane_a, ring_a, halves_a, parts_b, plane_b, ring_b, halves_b,
    loaded, in_send, in_recv, across_send, across_recv, forward_send, out_send, out_recv, box_send, box_recv,
    cs_a, cr_a, ps_a, pr_a, rs_a, rr_a, cs_b, cr_b, ps_b, pr_b, rs_b, rr_b,
):
    loads = [
        pltpu.make_async_copy(src, dst, loaded.at[n])
        for n, (src, dst) in enumerate(((points_in, points), (scales_in, scales), (noise_in, noise), (targets_in, targets)))
    ]
    for load in loads:
        load.start()
    barrier = pltpu.get_barrier_semaphore()

    def greet(device):
        pl.semaphore_signal(barrier, inc=1, device_id=device, device_id_type=MESH)

    def greet_plane(k, _):
        greet(in_plane(k))
        return 0

    for k in (8, -7, 7, -6, 6, -5, 5, -4, 4, -3, 3, -2, 2, -1, 1):
        greet(along_z(k))
    lax.fori_loop(1, PLANE, greet_plane, 0, unroll=True)
    greet(other_core())

    for load in loads:
        load.wait()
    goals = targets[...]
    scaled = (points[...] / scales[...]).astype(jnp.bfloat16)
    own[...] = scaled
    near_far[0, 0:BLOCK] = scaled
    near_far[0, BLOCK : BLOCK + RHS] = goals.astype(jnp.bfloat16)
    norms[0:BLOCK] = norm_lanes(scaled, 0)
    out_points[15 * BLOCK : 16 * BLOCK, 0:BLOCK] = scaled * -2.0
    out_points[15 * BLOCK : 16 * BLOCK, BLOCK:PAIR] = norm_lanes(scaled, 3)
    first_sum = Sum(parts_a, plane_a, ring_a, halves_a, (cs_a, cr_a, ps_a, pr_a, rs_a, rr_a))
    last_sum = Sum(parts_b, plane_b, ring_b, halves_b, (cs_b, cr_b, ps_b, pr_b, rs_b, rr_b))
    first_part = wide(gram(goals, goals))

    pl.semaphore_wait(barrier, (RING - 1) + (PLANE - 1) + 1)

    for step in DIRECT:
        i = OFFSETS.index(step)
        remote(near_far.at[0], near_far.at[2 * i], in_send.at[i], in_recv.at[i], along_z(step)).start()

    def across(i):
        remote(near_far.at[2 * i], near_far.at[2 * i + 1], across_send.at[i], across_recv.at[i], other_core()).start()

    def send_out(n, _):
        k, slot = back(n), 15 - n
        remote(own, out_raw.at[slot], out_send.at[k], out_recv.at[slot], in_plane(k)).start()
        return 0

    first_sum.begin(first_part)
    lax.fori_loop(1, PLANE, send_out, 0, unroll=True)
    across(0)

    def arrived(i):
        landed(near_far.at[2 * i], in_recv.at[i])
        across(i)

    def take(slot):
        norms[slot * BLOCK : (slot + 1) * BLOCK] = norm_lanes(near_far[slot, 0:BLOCK], 0)

    forwards = []

    def pass_on(step):
        i = OFFSETS.index(step)
        for more in FORWARD.get(step, ()):
            j = OFFSETS.index(step + more)
            n = len(forwards)
            forwards.append(j)
            remote(near_far.at[2 * i], near_far.at[2 * j], forward_send.at[n], in_recv.at[j], along_z(more)).start()
        take(2 * i)

    def take_across(steps):
        for step in steps:
            i = OFFSETS.index(step)
            landed(near_far.at[2 * i + 1], across_recv.at[i])
            take(2 * i + 1)

    def take_out(slot):
        landed(out_raw.at[slot], out_recv.at[slot])
        rows = out_raw[slot]
        at = pl.ds(pl.multiple_of(slot * BLOCK, BLOCK), BLOCK)
        out_points[at, 0:BLOCK] = rows * -2.0
        out_points[at, BLOCK:PAIR] = norm_lanes(rows, 3)

    def take_pair(o):
        take_out(2 * o)

        @pl.when(o < PAIRS - 1)
        def _():
            take_out(2 * o + 1)

    def sweep(steps, begin, end, finish, order, prepare=None):
        low = 2 * OFFSETS.index(steps[0])
        high = low + 2 * len(steps)
        size = (high - low) * BLOCK

        def ahead(o):
            rows = near_far[low:high, 0:BLOCK].reshape(size, BLOCK)
            at = pl.ds(pl.multiple_of(o * PAIR, PAIR), PAIR)
            return distances(rows, norms[low * BLOCK : high * BLOCK], out_points[at, :])

        def one(n, slot):
            o, later = order(n), order(jnp.minimum(n + 1, PAIRS - 1))
            if prepare is not None:
                pl.when(n < PAIRS - 1)(lambda: prepare(later))
            following = ahead(later)
            dirs = jnp.concatenate([near_far[s, BLOCK : BLOCK + RHS] for s in range(low, high)], axis=1)
            value = jnp.dot(dirs, matern(dist_sq[slot, 0:size]), preferred_element_type=jnp.float32)
            dist_sq[1 - slot, 0:size] = following
            finish(o, value)

        def two(h, _):
            one(2 * h, 0)
            one(2 * h + 1, 1)
            return 0

        if begin == 0:
            if prepare is not None:
                prepare(order(0))
            dist_sq[0, 0:size] = ahead(order(0))
        lax.fori_loop(begin // 2, end // 2, two, 0)

    def start_total(o, value):
        total[o] = value

    def add_total(o, value):
        total[o] += value

    def post(o, value):
        value = total[o] + value
        outbox[2 * o] = value[:, 0:BLOCK]
        outbox[2 * o + 1] = value[:, BLOCK:PAIR]

        def send(slot):
            remote(outbox.at[slot], inbox.at[slot], box_send.at[slot], box_recv, in_plane(15 - slot)).start()

        send(2 * o)

        @pl.when(o < PAIRS - 1)
        def _():
            send(2 * o + 1)

    def up(n):
        return n

    def down(n):
        return PAIRS - 1 - n

    def receive(steps):
        for step in steps:
            arrived(OFFSETS.index(step))
            pass_on(step)

    first_sum.over_plane()
    receive((3, -3, 1, -1))
    take_across(NEAR)
    sweep(NEAR, 0, 6, start_total, down, take_pair)
    receive((2, -2, 4, -4))
    first_sum.over_ring()
    sweep(NEAR, 6, PAIRS, start_total, down, take_pair)
    receive((6, -6))
    take_across(MIDDLE)
    sweep(MIDDLE, 0, PAIRS, add_total, up)
    first_sum.over_cores()
    receive(FAR)
    take_across(FAR)
    sweep(FAR, 0, PAIRS, post, up)

    lane = lax.broadcasted_iota(jnp.int32, (RHS, 128), 1)
    row = lax.broadcasted_iota(jnp.int32, (RHS, 128), 0)
    first = jnp.where(lane < RHS, first_sum.end(), 0.0)
    identity = jnp.where(lane == row + RHS, 1.0, 0.0)
    first_inverse = shift(eliminate(first + identity), -RHS)[:, 0:RHS]

    landed(inbox.at[pl.ds(0, PLANE - 1)], box_recv)
    image = (jnp.sum(inbox[0 : PLANE - 1], axis=0) + outbox[PLANE - 1]) + noise[...] * goals

    last_sum.begin(wide(gram(image, jnp.concatenate([goals, image], axis=0))))
    last_sum.over_plane()
    last_sum.over_ring()
    last_sum.over_cores()
    sums = last_sum.end()
    turned = sums[:, 0:RHS]
    curvature = wide(0.5 * (turned + turned.T))
    solved = eliminate(curvature + shift(first, RHS))
    step_matrix = shift(solved, -RHS)[:, 0:RHS]
    step_turned = step_matrix.T
    moved = precise(step_turned, jnp.concatenate([goals, image], axis=1))
    residual = goals - moved[:, 128:256]
    out_ref[0] = moved[:, 0:128]
    out_ref[1] = residual
    both = precise(step_turned, sums)
    cross = both[:, 0:RHS]
    square = precise(shift(both, -RHS)[:, 0:RHS], step_matrix)
    norm_new = first[:, 0:RHS] - cross - cross.T + square
    ratio_turned = precise(norm_new, first_inverse)
    out_ref[2] = residual + precise(ratio_turned, goals)

    for i, step in enumerate(OFFSETS):
        if step in DIRECT:
            landed(near_far.at[0], in_send.at[i])
        landed(near_far.at[0], across_send.at[i])
    for n in range(len(forwards)):
        landed(near_far.at[0], forward_send.at[n])
    for k in range(1, PLANE):
        landed(own, out_send.at[k])
        landed(outbox.at[0], box_send.at[k - 1])
    first_sum.sent()
    last_sum.sent()


def per_device(points, lengthscales, noise, targets):
    dma = pltpu.SemaphoreType.DMA
    sums = [
        pltpu.VMEM((3, 8, 128), jnp.float32),
        pltpu.VMEM((PLANE, 8, 128), jnp.float32),
        pltpu.VMEM((RING, 8, 128), jnp.float32),
        pltpu.VMEM((2, 8, 128), jnp.float32),
    ]
    sum_sems = [dma((2,)), dma((2,)), dma((PLANE,)), dma, dma((RING,)), dma]
    slots = 2 * len(OFFSETS)
    outs = pl.pallas_call(
        kernel,
        out_shape=jax.ShapeDtypeStruct((3, RHS, BLOCK), jnp.float32),
        in_specs=[pl.BlockSpec(memory_space=pltpu.HBM)] * 4,
        out_specs=pl.BlockSpec(memory_space=pltpu.VMEM),
        scratch_shapes=[
            pltpu.VMEM((BLOCK, BLOCK), jnp.float32),
            pltpu.VMEM((1, BLOCK), jnp.float32),
            pltpu.VMEM((1, BLOCK), jnp.float32),
            pltpu.VMEM((RHS, BLOCK), jnp.float32),
            pltpu.VMEM((2, 2 * len(MIDDLE) * BLOCK, PAIR), jnp.float32),
            pltpu.VMEM((slots, BLOCK + RHS, BLOCK), jnp.bfloat16),
            pltpu.VMEM((slots * BLOCK, BLOCK), jnp.bfloat16),
            pltpu.VMEM((PLANE, BLOCK, BLOCK), jnp.bfloat16),
            pltpu.VMEM((PLANE * BLOCK, PAIR), jnp.bfloat16),
            pltpu.VMEM((BLOCK, BLOCK), jnp.bfloat16),
            pltpu.VMEM((PAIRS, RHS, PAIR), jnp.float32),
            pltpu.VMEM((PLANE, RHS, BLOCK), jnp.float32),
            pltpu.VMEM((PLANE, RHS, BLOCK), jnp.float32),
            *sums,
            *sums,
            dma((4,)),
            dma((len(OFFSETS),)),
            dma((len(OFFSETS),)),
            dma((len(OFFSETS),)),
            dma((len(OFFSETS),)),
            dma((16,)),
            dma((PLANE,)),
            dma((PLANE,)),
            dma((PLANE,)),
            dma,
            *sum_sems,
            *sum_sems,
        ],
        compiler_params=pltpu.CompilerParams(collective_id=0, has_side_effects=True, vmem_limit_bytes=60 << 20),
        cost_estimate=pl.CostEstimate(flops=3 << 30, bytes_accessed=1 << 20, transcendentals=1 << 24),
        name="step",
    )(points, lengthscales[None, :], noise[None, :], targets)
    return outs[0], outs[1], outs[2]


def solution(mesh):
    spread = P(None, ("row", "col"))
    return jax.shard_map(
        per_device,
        mesh=mesh,
        in_specs=(P(("row", "col"), None), P(), P(("row", "col")), spread),
        out_specs=(spread, spread, spread),
        check_vma=False,
    )
```

```python
import functools

import jax
import jax.numpy as jnp
from jax import lax
from jax.experimental import pallas as pl
from jax.experimental.pallas import tpu as pltpu
from jax.sharding import PartitionSpec as P

MESH = pl.DeviceIdType.MESH
HI = lax.Precision.HIGHEST
root_five = 5.0**0.5
log2_e = 1.4426950408889634

PLANE = 16
RING = 16
BLOCK = 128
RHS = 32
DIRECT = (3, -3, 1, -1)
NEAR = (0, 1, -1, 3, -3)
MIDDLE = (2, -2, 4, -4, 6, -6)
FAR = (5, -5, 7, -7, 8)
OFFSETS = NEAR + MIDDLE + FAR
FORWARD = {3: (3, 1, -1), -3: (-3, -1, 1), 6: (2, 1, -1), -6: (-1, 1)}
PAIR = 2 * BLOCK
PAIRS = PLANE // 2


def place():
    row, col = lax.axis_index("row"), lax.axis_index("col")
    return lax.div(row, 8), lax.rem(lax.div(row, 2), 4), lax.rem(row, 2), col


def in_plane(step):
    y, x, core, z = place()
    y = lax.rem(y + lax.div(step, 4), 4)
    x = lax.rem(x + lax.rem(step, 4), 4)
    return (y * 8 + x * 2 + core, z)


def back(step):
    return lax.rem(4 - lax.div(step, 4), 4) * 4 + lax.rem(4 - lax.rem(step, 4), 4)


def along_z(step):
    y, x, core, z = place()
    return (y * 8 + x * 2 + core, lax.rem(z + (step + RING), RING))


def other_core():
    y, x, core, z = place()
    return (y * 8 + x * 2 + 1 - core, z)


def remote(src, dst, send, recv, device):
    return pltpu.make_async_remote_copy(
        src_ref=src, dst_ref=dst, send_sem=send, recv_sem=recv, device_id=device, device_id_type=MESH
    )


def landed(ref, sem):
    pltpu.make_async_copy(ref, ref, sem).wait()


def split_norms(rows):
    wide = rows.astype(jnp.float32)
    norm = jnp.sum(wide * wide, axis=1, keepdims=True)
    high = norm.astype(jnp.bfloat16).astype(jnp.float32)
    rest = norm - high
    middle = rest.astype(jnp.bfloat16).astype(jnp.float32)
    return high, middle, rest - middle


def norm_lanes(rows, first):
    high, middle, low = split_norms(rows)
    lane = lax.broadcasted_iota(jnp.int32, rows.shape, 1)
    ones = 3 - first
    value = jnp.where((lane >= ones) & (lane < ones + 3), 1.0, 0.0)
    value = jnp.where(lane == first, high, value)
    value = jnp.where(lane == first + 1, middle, value)
    return jnp.where(lane == first + 2, low, value).astype(jnp.bfloat16)


def matern(dist_sq):
    dist_sq = jnp.maximum(dist_sq, 1e-30)
    dist = dist_sq * lax.rsqrt(dist_sq)
    decay = jnp.exp2(dist * (-root_five * log2_e))
    return (((5.0 / 3.0 * dist_sq + 1.0) + root_five * dist) * decay).astype(jnp.bfloat16)


def distances(rows, norms, out_points):
    return lax.dot_general(
        jnp.concatenate([rows, norms], axis=1), out_points, (((1,), (1,)), ((), ())), preferred_element_type=jnp.float32
    )


def eliminate(matrix):
    parts = [matrix[8 * i : 8 * i + 8] for i in range(RHS // 8)]
    row = lax.broadcasted_iota(jnp.int32, parts[0].shape, 0)
    for k in range(0, RHS, 2):
        q, r = k // 8, k % 8
        left = [jnp.broadcast_to(part[:, k : k + 1], part.shape) for part in parts]
        right = [jnp.broadcast_to(part[:, k + 1 : k + 2], part.shape) for part in parts]
        upper, lower = parts[q][r : r + 1], parts[q][r + 1 : r + 2]
        a, b = left[q][r : r + 1], right[q][r : r + 1]
        c, d = left[q][r + 1 : r + 2], right[q][r + 1 : r + 2]
        scale = 1.0 / (a * d - b * c)
        upper, lower = (d * upper - b * lower) * scale, (a * lower - c * upper) * scale
        parts = [part - x * upper - y * lower for part, x, y in zip(parts, left, right)]
        parts[q] = jnp.where(row == r, upper, jnp.where(row == r + 1, lower, parts[q]))
    return jnp.concatenate(parts, axis=0)


def shift(value, lanes):
    return pltpu.roll(value, lanes % 128, 1)


def precise(left, right):
    return jnp.dot(left, right, precision=HI, preferred_element_type=jnp.float32)


def gram(left, right):
    return lax.dot_general(left, right, (((1,), (1,)), ((), ())), precision=HI, preferred_element_type=jnp.float32)


def pack(rows):
    lane = lax.broadcasted_iota(jnp.int32, (8, 128), 1)
    return jnp.where(lane < 64, rows[0:8], shift(rows[8:16], 64))


def wide(value):
    return jnp.concatenate([value, jnp.zeros((value.shape[0], 128 - value.shape[1]), value.dtype)], axis=1)


class Sum:
    def __init__(self, parts, plane, ring, halves, sems):
        self.parts, self.plane, self.ring, self.halves = parts, plane, ring, halves
        self.core_send, self.core_recv, self.plane_send, self.plane_recv, self.ring_send, self.ring_recv = sems

    def begin(self, value):
        core = place()[2]
        first, second = pack(value[0:16]), pack(value[16:32])
        low = core == 0
        self.parts[0] = jnp.where(low, first, second)
        self.parts[1] = jnp.where(low, second, first)
        remote(self.parts.at[1], self.parts.at[2], self.core_send.at[0], self.core_recv.at[0], other_core()).start()

    def over_plane(self):
        y, x, _, _ = place()
        me = y * 4 + x
        landed(self.parts.at[2], self.core_recv.at[0])
        self.plane[me] = self.parts[0] + self.parts[2]

        def send(k, _):
            remote(self.plane.at[me], self.plane.at[me], self.plane_send, self.plane_recv, in_plane(k)).start()
            return 0

        lax.fori_loop(1, PLANE, send, 0, unroll=True)

    def over_ring(self):
        me = place()[3]
        landed(self.plane.at[pl.ds(1, PLANE - 1)], self.plane_recv)
        self.ring[me] = jnp.sum(self.plane[...], axis=0)
        for k in (8, -7, 7, -6, 6, -5, 5, -4, 4, -3, 3, -2, 2, -1, 1):
            remote(self.ring.at[me], self.ring.at[me], self.ring_send, self.ring_recv, along_z(k)).start()

    def over_cores(self):
        core = place()[2]
        landed(self.ring.at[pl.ds(1, RING - 1)], self.ring_recv)
        self.halves[core] = jnp.sum(self.ring[...], axis=0)
        remote(self.halves.at[core], self.halves.at[core], self.core_send.at[1], self.core_recv.at[1], other_core()).start()

    def end(self):
        landed(self.halves.at[0], self.core_recv.at[1])
        first, second = self.halves[0], self.halves[1]
        return jnp.concatenate([first, shift(first, 64), second, shift(second, 64)], axis=0)

    def sent(self):
        landed(self.parts.at[1], self.core_send.at[0])
        landed(self.halves.at[0], self.core_send.at[1])
        landed(self.plane.at[pl.ds(1, PLANE - 1)], self.plane_send)
        landed(self.ring.at[pl.ds(1, RING - 1)], self.ring_send)


def kernel(
    points_in, scales_in, noise_in, targets_in, out_ref,
    points, scales, noise, targets, dist_sq, near_far, norms, out_raw, out_points, own, total, outbox, inbox,
    parts_a, plane_a, ring_a, halves_a, parts_b, plane_b, ring_b, halves_b,
    loaded, in_send, in_recv, across_send, across_recv, out_send, out_recv, box_send, box_recv,
    cs_a, cr_a, ps_a, pr_a, rs_a, rr_a, cs_b, cr_b, ps_b, pr_b, rs_b, rr_b,
):
    loads = [
        pltpu.make_async_copy(src, dst, loaded.at[n])
        for n, (src, dst) in enumerate(((points_in, points), (scales_in, scales), (noise_in, noise), (targets_in, targets)))
    ]
    for load in loads:
        load.start()
    barrier = pltpu.get_barrier_semaphore()

    def greet(device):
        pl.semaphore_signal(barrier, inc=1, device_id=device, device_id_type=MESH)

    def greet_plane(k, _):
        greet(in_plane(k))
        return 0

    for k in (8, -7, 7, -6, 6, -5, 5, -4, 4, -3, 3, -2, 2, -1, 1):
        greet(along_z(k))
    lax.fori_loop(1, PLANE, greet_plane, 0, unroll=True)
    greet(other_core())

    for load in loads:
        load.wait()
    goals = targets[...]
    scaled = (points[...] / scales[...]).astype(jnp.bfloat16)
    own[...] = scaled
    near_far[0, 0:BLOCK] = scaled
    near_far[0, BLOCK : BLOCK + RHS] = goals.astype(jnp.bfloat16)
    norms[0:BLOCK] = norm_lanes(scaled, 0)
    out_points[15 * BLOCK : 16 * BLOCK, 0:BLOCK] = scaled * -2.0
    out_points[15 * BLOCK : 16 * BLOCK, BLOCK:PAIR] = norm_lanes(scaled, 3)
    first_sum = Sum(parts_a, plane_a, ring_a, halves_a, (cs_a, cr_a, ps_a, pr_a, rs_a, rr_a))
    last_sum = Sum(parts_b, plane_b, ring_b, halves_b, (cs_b, cr_b, ps_b, pr_b, rs_b, rr_b))
    first_part = wide(gram(goals, goals))

    pl.semaphore_wait(barrier, (RING - 1) + (PLANE - 1) + 1)

    for step in DIRECT:
        i = OFFSETS.index(step)
        remote(near_far.at[0], near_far.at[2 * i], in_send, in_recv.at[i], along_z(step)).start()

    def across(i):
        remote(near_far.at[2 * i], near_far.at[2 * i + 1], across_send, across_recv.at[i], other_core()).start()

    def send_out(n, _):
        k, slot = back(n), 15 - n
        remote(own, out_raw.at[slot], out_send, out_recv.at[slot], in_plane(k)).start()
        return 0

    first_sum.begin(first_part)
    lax.fori_loop(1, PLANE, send_out, 0, unroll=True)
    across(0)

    def arrived(i):
        landed(near_far.at[2 * i], in_recv.at[i])
        across(i)

    def take(slot):
        norms[slot * BLOCK : (slot + 1) * BLOCK] = norm_lanes(near_far[slot, 0:BLOCK], 0)

    def pass_on(step):
        i = OFFSETS.index(step)
        for more in FORWARD.get(step, ()):
            j = OFFSETS.index(step + more)
            remote(near_far.at[2 * i], near_far.at[2 * j], in_send, in_recv.at[j], along_z(more)).start()
        take(2 * i)

    def take_across(steps):
        for step in steps:
            i = OFFSETS.index(step)
            landed(near_far.at[2 * i + 1], across_recv.at[i])
            take(2 * i + 1)

    def take_out(slot):
        landed(out_raw.at[slot], out_recv.at[slot])
        rows = out_raw[slot]
        at = pl.ds(pl.multiple_of(slot * BLOCK, BLOCK), BLOCK)
        out_points[at, 0:BLOCK] = rows * -2.0
        out_points[at, BLOCK:PAIR] = norm_lanes(rows, 3)

    def take_pair(o):
        take_out(2 * o)

        @pl.when(o < PAIRS - 1)
        def _():
            take_out(2 * o + 1)

    def sweep(steps, begin, end, finish, order, prepare=None):
        low = 2 * OFFSETS.index(steps[0])
        high = low + 2 * len(steps)
        size = (high - low) * BLOCK

        def ahead(o):
            rows = near_far[low:high, 0:BLOCK].reshape(size, BLOCK)
            at = pl.ds(pl.multiple_of(o * PAIR, PAIR), PAIR)
            return distances(rows, norms[low * BLOCK : high * BLOCK], out_points[at, :])

        def one(n, slot):
            o, later = order(n), order(jnp.minimum(n + 1, PAIRS - 1))
            if prepare is not None:
                pl.when(n < PAIRS - 1)(lambda: prepare(later))
            following = ahead(later)
            dirs = jnp.concatenate([near_far[s, BLOCK : BLOCK + RHS] for s in range(low, high)], axis=1)
            value = jnp.dot(dirs, matern(dist_sq[slot, 0:size]), preferred_element_type=jnp.float32)
            dist_sq[1 - slot, 0:size] = following
            finish(o, value)

        def two(h, _):
            one(2 * h, 0)
            one(2 * h + 1, 1)
            return 0

        if begin == 0:
            if prepare is not None:
                prepare(order(0))
            dist_sq[0, 0:size] = ahead(order(0))
        lax.fori_loop(begin // 2, end // 2, two, 0)

    def start_total(o, value):
        total[o] = value

    def add_total(o, value):
        total[o] += value

    def post(o, value):
        value = total[o] + value
        outbox[2 * o] = value[:, 0:BLOCK]
        outbox[2 * o + 1] = value[:, BLOCK:PAIR]

        def send(slot):
            remote(outbox.at[slot], inbox.at[slot], box_send, box_recv, in_plane(15 - slot)).start()

        send(2 * o)

        @pl.when(o < PAIRS - 1)
        def _():
            send(2 * o + 1)

    def up(n):
        return n

    def down(n):
        return PAIRS - 1 - n

    def receive(steps):
        for step in steps:
            arrived(OFFSETS.index(step))
            pass_on(step)

    first_sum.over_plane()
    receive((3, -3, 1, -1))
    take_across(NEAR)
    sweep(NEAR, 0, 4, start_total, down, take_pair)
    receive((2, -2, 4, -4))
    first_sum.over_ring()
    sweep(NEAR, 4, 6, start_total, down, take_pair)
    receive((6, -6))
    sweep(NEAR, 6, PAIRS, start_total, down, take_pair)
    take_across(MIDDLE)
    sweep(MIDDLE, 0, PAIRS, add_total, up)
    first_sum.over_cores()
    receive(FAR)
    take_across(FAR)
    sweep(FAR, 0, PAIRS, post, up)

    lane = lax.broadcasted_iota(jnp.int32, (RHS, 128), 1)
    row = lax.broadcasted_iota(jnp.int32, (RHS, 128), 0)
    first = jnp.where(lane < RHS, first_sum.end(), 0.0)
    identity = jnp.where(lane == row + RHS, 1.0, 0.0)
    first_inverse = shift(eliminate(first + identity), -RHS)[:, 0:RHS]

    landed(inbox.at[pl.ds(0, PLANE - 1)], box_recv)
    image = (jnp.sum(inbox[0 : PLANE - 1], axis=0) + outbox[PLANE - 1]) + noise[...] * goals

    last_sum.begin(wide(gram(image, jnp.concatenate([goals, image], axis=0))))
    last_sum.over_plane()
    last_sum.over_ring()
    last_sum.over_cores()
    sums = last_sum.end()
    turned = sums[:, 0:RHS]
    curvature = wide(0.5 * (turned + turned.T))
    solved = eliminate(curvature + shift(first, RHS))
    step_matrix = shift(solved, -RHS)[:, 0:RHS]
    step_turned = step_matrix.T
    moved = precise(step_turned, jnp.concatenate([goals, image], axis=1))
    residual = goals - moved[:, 128:256]
    out_ref[0] = moved[:, 0:128]
    out_ref[1] = residual
    both = precise(step_turned, sums)
    cross = both[:, 0:RHS]
    square = precise(shift(both, -RHS)[:, 0:RHS], step_matrix)
    norm_new = first[:, 0:RHS] - cross - cross.T + square
    ratio_turned = precise(norm_new, first_inverse)
    out_ref[2] = residual + precise(ratio_turned, goals)

    landed(near_far.at[pl.ds(0, len(OFFSETS) - 1)], in_send)
    landed(near_far.at[pl.ds(0, len(OFFSETS))], across_send)
    landed(out_raw.at[pl.ds(0, PLANE - 1)], out_send)
    landed(outbox.at[pl.ds(0, PLANE - 1)], box_send)
    first_sum.sent()
    last_sum.sent()


def per_device(points, lengthscales, noise, targets):
    dma = pltpu.SemaphoreType.DMA
    sums = [
        pltpu.VMEM((3, 8, 128), jnp.float32),
        pltpu.VMEM((PLANE, 8, 128), jnp.float32),
        pltpu.VMEM((RING, 8, 128), jnp.float32),
        pltpu.VMEM((2, 8, 128), jnp.float32),
    ]
    sum_sems = [dma((2,)), dma((2,)), dma, dma, dma, dma]
    slots = 2 * len(OFFSETS)
    outs = pl.pallas_call(
        kernel,
        out_shape=jax.ShapeDtypeStruct((3, RHS, BLOCK), jnp.float32),
        in_specs=[pl.BlockSpec(memory_space=pltpu.HBM)] * 4,
        out_specs=pl.BlockSpec(memory_space=pltpu.VMEM),
        scratch_shapes=[
            pltpu.VMEM((BLOCK, BLOCK), jnp.float32),
            pltpu.VMEM((1, BLOCK), jnp.float32),
            pltpu.VMEM((1, BLOCK), jnp.float32),
            pltpu.VMEM((RHS, BLOCK), jnp.float32),
            pltpu.VMEM((2, 2 * len(MIDDLE) * BLOCK, PAIR), jnp.float32),
            pltpu.VMEM((slots, BLOCK + RHS, BLOCK), jnp.bfloat16),
            pltpu.VMEM((slots * BLOCK, BLOCK), jnp.bfloat16),
            pltpu.VMEM((PLANE, BLOCK, BLOCK), jnp.bfloat16),
            pltpu.VMEM((PLANE * BLOCK, PAIR), jnp.bfloat16),
            pltpu.VMEM((BLOCK, BLOCK), jnp.bfloat16),
            pltpu.VMEM((PAIRS, RHS, PAIR), jnp.float32),
            pltpu.VMEM((PLANE, RHS, BLOCK), jnp.float32),
            pltpu.VMEM((PLANE, RHS, BLOCK), jnp.float32),
            *sums,
            *sums,
            dma((4,)),
            dma,
            dma((len(OFFSETS),)),
            dma,
            dma((len(OFFSETS),)),
            dma,
            dma((PLANE,)),
            dma,
            dma,
            *sum_sems,
            *sum_sems,
        ],
        compiler_params=pltpu.CompilerParams(collective_id=0, has_side_effects=True, vmem_limit_bytes=60 << 20),
        cost_estimate=pl.CostEstimate(flops=3 << 30, bytes_accessed=1 << 20, transcendentals=1 << 24),
        name="step",
    )(points, lengthscales[None, :], noise[None, :], targets)
    return outs[0], outs[1], outs[2]


def solution(mesh):
    spread = P(None, ("row", "col"))
    return jax.shard_map(
        per_device,
        mesh=mesh,
        in_specs=(P(("row", "col"), None), P(), P(("row", "col")), spread),
        out_specs=(spread, spread, spread),
        check_vma=False,
    )
```

```python
import functools

import jax
import jax.numpy as jnp
from jax import lax
from jax.experimental import pallas as pl
from jax.experimental.pallas import tpu as pltpu
from jax.sharding import PartitionSpec as P

MESH = pl.DeviceIdType.MESH
HI = lax.Precision.HIGHEST
root_five = 5.0**0.5
log2_e = 1.4426950408889634

PLANE = 16
RING = 16
BLOCK = 128
RHS = 32
DIRECT = (3, -3, 1, -1)
NEAR = (0, 1, -1, 3, -3)
MIDDLE = (2, -2, 4, -4, 6, -6)
FAR = (5, -5, 7, -7, 8)
OFFSETS = NEAR + MIDDLE + FAR
FORWARD = {3: (3, 1, -1), -3: (-3, -1, 1), 6: (2, 1, -1), -6: (-1, 1)}
PAIR = 2 * BLOCK
PAIRS = PLANE // 2


def place():
    row, col = lax.axis_index("row"), lax.axis_index("col")
    return lax.div(row, 8), lax.rem(lax.div(row, 2), 4), lax.rem(row, 2), col


def in_plane(step):
    y, x, core, z = place()
    y = lax.rem(y + lax.div(step, 4), 4)
    x = lax.rem(x + lax.rem(step, 4), 4)
    return (y * 8 + x * 2 + core, z)


def back(step):
    return lax.rem(4 - lax.div(step, 4), 4) * 4 + lax.rem(4 - lax.rem(step, 4), 4)


def along_z(step):
    y, x, core, z = place()
    return (y * 8 + x * 2 + core, lax.rem(z + (step + RING), RING))


def other_core():
    y, x, core, z = place()
    return (y * 8 + x * 2 + 1 - core, z)


def remote(src, dst, send, recv, device):
    return pltpu.make_async_remote_copy(
        src_ref=src, dst_ref=dst, send_sem=send, recv_sem=recv, device_id=device, device_id_type=MESH
    )


def landed(ref, sem):
    pltpu.make_async_copy(ref, ref, sem).wait()


def split_norms(rows):
    wide = rows.astype(jnp.float32)
    norm = jnp.sum(wide * wide, axis=1, keepdims=True)
    high = norm.astype(jnp.bfloat16).astype(jnp.float32)
    rest = norm - high
    middle = rest.astype(jnp.bfloat16).astype(jnp.float32)
    return high, middle, rest - middle


def norm_lanes(rows, first):
    high, middle, low = split_norms(rows)
    lane = lax.broadcasted_iota(jnp.int32, rows.shape, 1)
    ones = 3 - first
    value = jnp.where((lane >= ones) & (lane < ones + 3), 1.0, 0.0)
    value = jnp.where(lane == first, high, value)
    value = jnp.where(lane == first + 1, middle, value)
    return jnp.where(lane == first + 2, low, value).astype(jnp.bfloat16)


def matern(dist_sq):
    dist_sq = jnp.maximum(dist_sq, 1e-30)
    dist = dist_sq * lax.rsqrt(dist_sq)
    decay = jnp.exp2(dist * (-root_five * log2_e))
    return (((5.0 / 3.0 * dist_sq + 1.0) + root_five * dist) * decay).astype(jnp.bfloat16)


def distances(rows, norms, out_points):
    return lax.dot_general(
        jnp.concatenate([rows, norms], axis=1), out_points, (((1,), (1,)), ((), ())), preferred_element_type=jnp.float32
    )


def eliminate(matrix):
    parts = [matrix[8 * i : 8 * i + 8] for i in range(RHS // 8)]
    row = lax.broadcasted_iota(jnp.int32, parts[0].shape, 0)
    for k in range(0, RHS, 2):
        q, r = k // 8, k % 8
        left = [jnp.broadcast_to(part[:, k : k + 1], part.shape) for part in parts]
        right = [jnp.broadcast_to(part[:, k + 1 : k + 2], part.shape) for part in parts]
        upper, lower = parts[q][r : r + 1], parts[q][r + 1 : r + 2]
        a, b = left[q][r : r + 1], right[q][r : r + 1]
        c, d = left[q][r + 1 : r + 2], right[q][r + 1 : r + 2]
        scale = 1.0 / (a * d - b * c)
        upper, lower = (d * upper - b * lower) * scale, (a * lower - c * upper) * scale
        parts = [part - x * upper - y * lower for part, x, y in zip(parts, left, right)]
        parts[q] = jnp.where(row == r, upper, jnp.where(row == r + 1, lower, parts[q]))
    return jnp.concatenate(parts, axis=0)


def shift(value, lanes):
    return pltpu.roll(value, lanes % 128, 1)


def precise(left, right):
    return jnp.dot(left, right, precision=HI, preferred_element_type=jnp.float32)


def gram(left, right):
    return lax.dot_general(left, right, (((1,), (1,)), ((), ())), precision=HI, preferred_element_type=jnp.float32)


def pack(rows):
    lane = lax.broadcasted_iota(jnp.int32, (8, 128), 1)
    return jnp.where(lane < 64, rows[0:8], shift(rows[8:16], 64))


def wide(value):
    return jnp.concatenate([value, jnp.zeros((value.shape[0], 128 - value.shape[1]), value.dtype)], axis=1)


class Sum:
    def __init__(self, parts, plane, ring, halves, sems):
        self.parts, self.plane, self.ring, self.halves = parts, plane, ring, halves
        self.core_send, self.core_recv, self.plane_send, self.plane_recv, self.ring_send, self.ring_recv = sems

    def begin(self, value):
        core = place()[2]
        first, second = pack(value[0:16]), pack(value[16:32])
        low = core == 0
        self.parts[0] = jnp.where(low, first, second)
        self.parts[1] = jnp.where(low, second, first)
        remote(self.parts.at[1], self.parts.at[2], self.core_send.at[0], self.core_recv.at[0], other_core()).start()

    def over_plane(self):
        y, x, _, _ = place()
        me = y * 4 + x
        landed(self.parts.at[2], self.core_recv.at[0])
        self.plane[me] = self.parts[0] + self.parts[2]

        def send(k, _):
            remote(self.plane.at[me], self.plane.at[me], self.plane_send, self.plane_recv, in_plane(k)).start()
            return 0

        lax.fori_loop(1, PLANE, send, 0, unroll=True)

    def over_ring(self):
        me = place()[3]
        landed(self.plane.at[pl.ds(1, PLANE - 1)], self.plane_recv)
        self.ring[me] = jnp.sum(self.plane[...], axis=0)
        for k in (8, -7, 7, -6, 6, -5, 5, -4, 4, -3, 3, -2, 2, -1, 1):
            remote(self.ring.at[me], self.ring.at[me], self.ring_send, self.ring_recv, along_z(k)).start()

    def over_cores(self):
        core = place()[2]
        landed(self.ring.at[pl.ds(1, RING - 1)], self.ring_recv)
        self.halves[core] = jnp.sum(self.ring[...], axis=0)
        remote(self.halves.at[core], self.halves.at[core], self.core_send.at[1], self.core_recv.at[1], other_core()).start()

    def end(self):
        landed(self.halves.at[0], self.core_recv.at[1])
        first, second = self.halves[0], self.halves[1]
        return jnp.concatenate([first, shift(first, 64), second, shift(second, 64)], axis=0)

    def sent(self):
        landed(self.parts.at[1], self.core_send.at[0])
        landed(self.halves.at[0], self.core_send.at[1])
        landed(self.plane.at[pl.ds(1, PLANE - 1)], self.plane_send)
        landed(self.ring.at[pl.ds(1, RING - 1)], self.ring_send)


def kernel(
    points_in, scales_in, noise_in, targets_in, out_ref,
    points, scales, noise, targets, dist_sq, near_far, norms, out_raw, out_points, own, total, outbox, inbox,
    parts_a, plane_a, ring_a, halves_a, parts_b, plane_b, ring_b, halves_b,
    loaded, in_send, in_recv, across_send, across_recv, out_send, out_recv, box_send, box_recv,
    cs_a, cr_a, ps_a, pr_a, rs_a, rr_a, cs_b, cr_b, ps_b, pr_b, rs_b, rr_b,
):
    loads = [
        pltpu.make_async_copy(src, dst, loaded.at[n])
        for n, (src, dst) in enumerate(((points_in, points), (scales_in, scales), (noise_in, noise), (targets_in, targets)))
    ]
    for load in loads:
        load.start()
    barrier = pltpu.get_barrier_semaphore()

    def greet(device):
        pl.semaphore_signal(barrier, inc=1, device_id=device, device_id_type=MESH)

    def greet_plane(k, _):
        greet(in_plane(k))
        return 0

    for k in (8, -7, 7, -6, 6, -5, 5, -4, 4, -3, 3, -2, 2, -1, 1):
        greet(along_z(k))
    lax.fori_loop(1, PLANE, greet_plane, 0, unroll=True)
    greet(other_core())

    for load in loads:
        load.wait()
    goals = targets[...]
    scaled = (points[...] / scales[...]).astype(jnp.bfloat16)
    own[...] = scaled
    near_far[0, 0:BLOCK] = scaled
    near_far[0, BLOCK : BLOCK + RHS] = goals.astype(jnp.bfloat16)
    norms[0:BLOCK] = norm_lanes(scaled, 0)
    out_points[15 * BLOCK : 16 * BLOCK, 0:BLOCK] = scaled * -2.0
    out_points[15 * BLOCK : 16 * BLOCK, BLOCK:PAIR] = norm_lanes(scaled, 3)
    first_sum = Sum(parts_a, plane_a, ring_a, halves_a, (cs_a, cr_a, ps_a, pr_a, rs_a, rr_a))
    last_sum = Sum(parts_b, plane_b, ring_b, halves_b, (cs_b, cr_b, ps_b, pr_b, rs_b, rr_b))
    first_part = wide(gram(goals, goals))

    pl.semaphore_wait(barrier, (RING - 1) + (PLANE - 1) + 1)

    for step in DIRECT:
        i = OFFSETS.index(step)
        remote(near_far.at[0], near_far.at[2 * i], in_send, in_recv.at[i], along_z(step)).start()

    def across(i):
        remote(near_far.at[2 * i], near_far.at[2 * i + 1], across_send, across_recv.at[i], other_core()).start()

    def send_out(n, _):
        k, slot = back(n), 15 - n
        remote(own, out_raw.at[slot], out_send, out_recv.at[slot], in_plane(k)).start()
        return 0

    lax.fori_loop(1, PLANE, send_out, 0, unroll=True)
    across(0)
    first_sum.begin(first_part)

    def arrived(i):
        landed(near_far.at[2 * i], in_recv.at[i])
        across(i)

    def take(slot):
        norms[slot * BLOCK : (slot + 1) * BLOCK] = norm_lanes(near_far[slot, 0:BLOCK], 0)

    def pass_on(step):
        i = OFFSETS.index(step)
        for more in FORWARD.get(step, ()):
            j = OFFSETS.index(step + more)
            remote(near_far.at[2 * i], near_far.at[2 * j], in_send, in_recv.at[j], along_z(more)).start()
        take(2 * i)

    def take_across(steps):
        for step in steps:
            i = OFFSETS.index(step)
            landed(near_far.at[2 * i + 1], across_recv.at[i])
            take(2 * i + 1)

    def take_out(slot):
        landed(out_raw.at[slot], out_recv.at[slot])
        rows = out_raw[slot]
        at = pl.ds(pl.multiple_of(slot * BLOCK, BLOCK), BLOCK)
        out_points[at, 0:BLOCK] = rows * -2.0
        out_points[at, BLOCK:PAIR] = norm_lanes(rows, 3)

    def take_pair(o):
        take_out(2 * o)

        @pl.when(o < PAIRS - 1)
        def _():
            take_out(2 * o + 1)

    def sweep(steps, finish, order, prepare=None, between=()):
        low = 2 * OFFSETS.index(steps[0])
        high = low + 2 * len(steps)
        size = (high - low) * BLOCK

        def ahead(o):
            rows = near_far[low:high, 0:BLOCK].reshape(size, BLOCK)
            at = pl.ds(pl.multiple_of(o * PAIR, PAIR), PAIR)
            return distances(rows, norms[low * BLOCK : high * BLOCK], out_points[at, :])

        def one(n, slot):
            o, later = order(n), order(jnp.minimum(n + 1, PAIRS - 1))
            if prepare is not None:
                pl.when(n < PAIRS - 1)(lambda: prepare(later))
            following = ahead(later)
            dirs = jnp.concatenate([near_far[s, BLOCK : BLOCK + RHS] for s in range(low, high)], axis=1)
            value = jnp.dot(dirs, matern(dist_sq[slot, 0:size]), preferred_element_type=jnp.float32)
            dist_sq[1 - slot, 0:size] = following
            finish(o, value)

        def two(h, _):
            for at in between:
                pl.when(h == at)(between[at])
            one(2 * h, 0)
            one(2 * h + 1, 1)
            return 0

        if prepare is not None:
            prepare(order(0))
        dist_sq[0, 0:size] = ahead(order(0))
        lax.fori_loop(0, PAIRS // 2, two, 0)

    def start_total(o, value):
        total[o] = value

    def add_total(o, value):
        total[o] += value

    def post(o, value):
        value = total[o] + value
        outbox[2 * o] = value[:, 0:BLOCK]
        outbox[2 * o + 1] = value[:, BLOCK:PAIR]

        def send(slot):
            remote(outbox.at[slot], inbox.at[slot], box_send, box_recv, in_plane(15 - slot)).start()

        send(2 * o)

        @pl.when(o < PAIRS - 1)
        def _():
            send(2 * o + 1)

    def up(n):
        return n

    def down(n):
        return PAIRS - 1 - n

    def receive(steps):
        for step in steps:
            arrived(OFFSETS.index(step))
            pass_on(step)

    receive((3, -3, 1, -1))
    first_sum.over_plane()
    take_across(NEAR)
    def after_four():
        receive((2, -2, 4, -4))
        first_sum.over_ring()

    def after_six():
        receive((6, -6))

    sweep(NEAR, start_total, down, take_pair, {2: after_four, 3: after_six})
    take_across(MIDDLE)
    sweep(MIDDLE, add_total, up)
    first_sum.over_cores()
    receive(FAR)
    take_across(FAR)
    sweep(FAR, post, up)

    lane = lax.broadcasted_iota(jnp.int32, (RHS, 128), 1)
    row = lax.broadcasted_iota(jnp.int32, (RHS, 128), 0)
    first = jnp.where(lane < RHS, first_sum.end(), 0.0)
    identity = jnp.where(lane == row + RHS, 1.0, 0.0)
    first_inverse = shift(eliminate(first + identity), -RHS)[:, 0:RHS]

    landed(inbox.at[pl.ds(0, PLANE - 1)], box_recv)
    image = (jnp.sum(inbox[0 : PLANE - 1], axis=0) + outbox[PLANE - 1]) + noise[...] * goals

    last_sum.begin(wide(gram(image, jnp.concatenate([goals, image], axis=0))))
    last_sum.over_plane()
    last_sum.over_ring()
    weighted = precise(first_inverse, goals)
    last_sum.over_cores()
    sums = last_sum.end()
    turned = sums[:, 0:RHS]
    curvature = wide(0.5 * (turned + turned.T))
    solved = eliminate(curvature + shift(first, RHS))
    step_matrix = shift(solved, -RHS)[:, 0:RHS]
    step_turned = step_matrix.T
    moved = precise(step_turned, jnp.concatenate([goals, image], axis=1))
    residual = goals - moved[:, 128:256]
    out_ref[0] = moved[:, 0:128]
    out_ref[1] = residual
    both = precise(step_turned, sums)
    cross = both[:, 0:RHS]
    square = precise(shift(both, -RHS)[:, 0:RHS], step_matrix)
    norm_new = first[:, 0:RHS] - cross - cross.T + square
    out_ref[2] = residual + precise(norm_new, weighted)

    landed(near_far.at[pl.ds(0, len(OFFSETS) - 1)], in_send)
    landed(near_far.at[pl.ds(0, len(OFFSETS))], across_send)
    landed(out_raw.at[pl.ds(0, PLANE - 1)], out_send)
    landed(outbox.at[pl.ds(0, PLANE - 1)], box_send)
    first_sum.sent()
    last_sum.sent()


def per_device(points, lengthscales, noise, targets):
    dma = pltpu.SemaphoreType.DMA
    sums = [
        pltpu.VMEM((3, 8, 128), jnp.float32),
        pltpu.VMEM((PLANE, 8, 128), jnp.float32),
        pltpu.VMEM((RING, 8, 128), jnp.float32),
        pltpu.VMEM((2, 8, 128), jnp.float32),
    ]
    sum_sems = [dma((2,)), dma((2,)), dma, dma, dma, dma]
    slots = 2 * len(OFFSETS)
    outs = pl.pallas_call(
        kernel,
        out_shape=jax.ShapeDtypeStruct((3, RHS, BLOCK), jnp.float32),
        in_specs=[pl.BlockSpec(memory_space=pltpu.HBM)] * 4,
        out_specs=pl.BlockSpec(memory_space=pltpu.VMEM),
        scratch_shapes=[
            pltpu.VMEM((BLOCK, BLOCK), jnp.float32),
            pltpu.VMEM((1, BLOCK), jnp.float32),
            pltpu.VMEM((1, BLOCK), jnp.float32),
            pltpu.VMEM((RHS, BLOCK), jnp.float32),
            pltpu.VMEM((2, 2 * len(MIDDLE) * BLOCK, PAIR), jnp.float32),
            pltpu.VMEM((slots, BLOCK + RHS, BLOCK), jnp.bfloat16),
            pltpu.VMEM((slots * BLOCK, BLOCK), jnp.bfloat16),
            pltpu.VMEM((PLANE, BLOCK, BLOCK), jnp.bfloat16),
            pltpu.VMEM((PLANE * BLOCK, PAIR), jnp.bfloat16),
            pltpu.VMEM((BLOCK, BLOCK), jnp.bfloat16),
            pltpu.VMEM((PAIRS, RHS, PAIR), jnp.float32),
            pltpu.VMEM((PLANE, RHS, BLOCK), jnp.float32),
            pltpu.VMEM((PLANE, RHS, BLOCK), jnp.float32),
            *sums,
            *sums,
            dma((4,)),
            dma,
            dma((len(OFFSETS),)),
            dma,
            dma((len(OFFSETS),)),
            dma,
            dma((PLANE,)),
            dma,
            dma,
            *sum_sems,
            *sum_sems,
        ],
        compiler_params=pltpu.CompilerParams(collective_id=0, has_side_effects=True, vmem_limit_bytes=60 << 20),
        cost_estimate=pl.CostEstimate(flops=3 << 30, bytes_accessed=1 << 20, transcendentals=1 << 24),
        name="step",
    )(points, lengthscales[None, :], noise[None, :], targets)
    return outs[0], outs[1], outs[2]


def solution(mesh):
    spread = P(None, ("row", "col"))
    return jax.shard_map(
        per_device,
        mesh=mesh,
        in_specs=(P(("row", "col"), None), P(), P(("row", "col")), spread),
        out_specs=(spread, spread, spread),
        check_vma=False,
    )
```
